32 devices in a mesh: groups: 2 (over x), gx: 16 (over z, y, core).
Axes of the slice: x: 2, y: 2, z: 4, core: 2. Of those that a mesh axis runs over, the one named last changes fastest.
Arguments:
- log_perm: float32 [512, 32, 128], P(('groups', 'gx')), parts along dimension 0, may hold values from -3 to 3
- saturation: float32 [512, 32, 128], P(('groups', 'gx')), parts along dimension 0, may hold values from 0.05 to 0.95
- porosity: float32 [512, 32, 128], P(('groups', 'gx')), parts along dimension 0, may hold values from 0.1 to 0.3
- source: float32 [512, 32, 128], P(('groups', 'gx')), parts along dimension 0, may hold values from -6 to 6
- support_bits: int32 [512, 32, 128], P(('groups', 'gx')), parts along dimension 0, may hold values from 1 to 255, as said below
Outputs:
- pressure: float32 [512, 32, 128], P(('groups', 'gx')), parts along dimension 0
- new_saturation: float32 [512, 32, 128], P(('groups', 'gx')), parts along dimension 0
The draws below stay inside these ranges and needn't reach their ends.
There are 2 independent parts, one for each index of `groups`. The reference program is written for one: setup_inputs(seed, part) draws one part's arguments, and reference() takes and returns one part's arrays. A program takes and returns all parts, laid end to end along the dimension named above; each array names one. Nothing has to cross between parts.
Inputs may be any that keep to these rules, and one draw needn't show every extreme that they name: `support_bits`: bit k of a cell's value, k = a + 2 b + 4 c, marks the cell as inside the basis support of its colour-k coarse node; the bit of the colour of the cell's own block is always set.
All inputs are finite; a program needn't handle non-finite values.
Results may differ from the reference program's by a relative error of at most 0.0003.
Values sent between devices are 32-bit elements; how exact they have to be, the bound alone decides.
No kernel may reach another device: no remote copies, remote signals or barrier semaphores. Data moves between devices by JAX's collectives and lax.ppermute only.
A program may use at most 64 MiB of HBM per device.

```python
import jax
import jax.numpy as jnp
from jax import lax

NY = 32
NZ = 128
BX = 16
BY = 16
BZ = 8
JACOBI = 2
CHEBY = 4
NX = 256
NCX = 16
NCY = 2
NCZ = 16


def draw_support_bits(key, part):
    first = jax.random.randint(jax.random.fold_in(key, 11), (NX, NY, NZ), 0, 256)
    second = jax.random.randint(jax.random.fold_in(key, 12), (NX, NY, NZ), 0, 256)
    home_x = jnp.arange(NX) // BX % 2
    home_y = jnp.arange(NY) // BY % 2
    home_z = jnp.arange(NZ) // BZ % 2
    home = home_x[:, None, None] + 2 * home_y[None, :, None] + 4 * home_z[None, None, :]
    merged = jnp.bitwise_or(jnp.bitwise_or(first, second), jnp.left_shift(jnp.ones_like(home), home))
    return merged.astype(jnp.int32)


def levels(rng, shape, cuts, smallest, top_value):
    factor_of = 1.0
    for position, shards_of in cuts:
        steps = jax.random.uniform(jax.random.fold_in(jax.random.fold_in(rng, 6), position), (shards_of,), jnp.float32, smallest / len(cuts), top_value / len(cuts))
        factor_of = factor_of * jnp.repeat(jnp.exp(steps), shape[position] // shards_of).reshape((-1,) + (1,) * (len(shape) - 1 - position))
    return factor_of


def normal_values(stream_key, shape, deviation, most, cuts=(), kind=jnp.bfloat16):
    result = deviation * jax.random.normal(stream_key, shape, jnp.float32)
    if cuts:
        result = result * levels(stream_key, shape, cuts, -0.22, 0.18)
    return jnp.clip(result, -most, most).astype(kind)


def setup_inputs(seed: int = 0, part: int = 0) -> dict:
    streams_of = jax.random.split(jax.random.key(seed), 6)
    part_keys = jax.random.split(jax.random.fold_in(streams_of[5], part), 6)
    log_perm = normal_values(part_keys[0], (NX, NY, NZ), 1.0, 3.0, ((0, 16),), jnp.float32)
    saturation = jnp.clip(0.05 + 0.9 * jax.random.uniform(part_keys[1], (NX, NY, NZ), jnp.float32) ** levels(part_keys[1], (NX, NY, NZ), ((0, 16),), -0.2, 0.2), 0.05, 0.95)
    porosity = jnp.clip(0.1 + 0.20000001043081284 * jax.random.uniform(part_keys[2], (NX, NY, NZ), jnp.float32) ** levels(part_keys[2], (NX, NY, NZ), ((0, 16),), -0.2, 0.2), 0.1, 0.3)
    source = normal_values(part_keys[3], (NX, NY, NZ), 1.0, 6.0, ((0, 16),), jnp.float32)
    support_bits = draw_support_bits(jax.random.fold_in(jax.random.fold_in(streams_of[5], part), 71), part)
    return dict(log_perm=log_perm, saturation=saturation, porosity=porosity, source=source, support_bits=support_bits)


water_viscosity = 1.0
oil_viscosity = 4.0
compress = 0.02
relax_weight = 2.0 / 3.0
courant = 0.5
upper_margin = 1.25
lower_share = 0.1
tiny_eps = 1e-06

def pad_axis(array, axis, before, after):
    widths = [(0, 0)] * array.ndim
    widths[axis] = (before, after)
    return jnp.pad(array, widths)

def spread(pair, axis):
    stacked = jnp.stack([pair[colour >> axis & 1] for colour in range(8)])
    if axis == 0:
        return stacked[:, :, None, None]
    if axis == 1:
        return stacked[:, None, :, None]
    return stacked[:, None, None, :]

def node_pair(coords, block):
    blocks = coords // block
    upper = coords % block >= block // 2
    beside = jnp.where(upper, blocks + 1, blocks - 1)
    return jnp.stack([jnp.where(blocks % 2 == parity, blocks, beside) for parity in range(2)])

def valid_pair(nodes, count):
    return ((nodes >= 0) & (nodes < count)).astype(jnp.float32)

def mobility(satur):
    return satur * satur / water_viscosity + (1.0 - satur) * (1.0 - satur) / oil_viscosity

def harmonic(left, right):
    return 2.0 * left * right / (left + right)

def coefficients(perm_ext, mob_ext, porous, face_ok):
    face_x = harmonic(perm_ext[:-1], perm_ext[1:]) * (0.5 * (mob_ext[:-1] + mob_ext[1:])) * face_ok
    perm_in = perm_ext[1:-1]
    mob_in = mob_ext[1:-1]
    face_y = harmonic(perm_in[:, :-1], perm_in[:, 1:]) * (0.5 * (mob_in[:, :-1] + mob_in[:, 1:]))
    face_z = harmonic(perm_in[:, :, :-1], perm_in[:, :, 1:]) * (0.5 * (mob_in[:, :, :-1] + mob_in[:, :, 1:]))
    links = (face_x[:-1], face_x[1:], pad_axis(face_y, 1, 1, 0), pad_axis(face_y, 1, 0, 1), pad_axis(face_z, 2, 1, 0), pad_axis(face_z, 2, 0, 1))
    diagonal = compress * porous + links[0] + links[1] + links[2] + links[3] + links[4] + links[5]
    return (face_x, face_y, face_z, links, diagonal)

def same_flags(nodes_x, nodes_y, nodes_z):
    faces_x = (nodes_x[:, :-1] == nodes_x[:, 1:]).astype(jnp.float32)
    faces_y = (nodes_y[:, :-1] == nodes_y[:, 1:]).astype(jnp.float32)
    faces_z = (nodes_z[:, :-1] == nodes_z[:, 1:]).astype(jnp.float32)
    return (spread(faces_x[:, :-1], 0), spread(faces_x[:, 1:], 0), spread(pad_axis(faces_y, 1, 1, 0), 1), spread(pad_axis(faces_y, 1, 0, 1), 1), spread(pad_axis(faces_z, 1, 1, 0), 2), spread(pad_axis(faces_z, 1, 0, 1), 2))

def home_basis(coords_x, coords_y, coords_z, inside):
    home = (coords_x // BX % 2)[:, None, None] + 2 * (coords_y // BY % 2)[None, :, None] + 4 * (coords_z // BZ % 2)[None, None, :]
    colours = jnp.arange(8, dtype=jnp.int32)[:, None, None, None]
    return (colours == home[None]).astype(jnp.float32) * inside[None, :, None, None]

def support_mask(bits, valid_x, valid_y, valid_z, inside):
    colours = jnp.arange(8, dtype=jnp.int32)[:, None, None, None]
    marked = jnp.bitwise_and(jnp.right_shift(bits[None], colours), 1).astype(jnp.float32)
    return marked * spread(valid_x, 0) * spread(valid_y, 1) * spread(valid_z, 2) * inside[None, :, None, None]

def jacobi_sweep(basis_ext, mask, diagonal, links, same, outside):
    centre = basis_ext[:, 1:-1]
    pull = links[0] * same[0] * basis_ext[:, :-2] + links[1] * same[1] * basis_ext[:, 2:]
    pull = pull + links[2] * same[2] * pad_axis(centre[:, :, :-1], 2, 1, 0) + links[3] * same[3] * pad_axis(centre[:, :, 1:], 2, 0, 1)
    pull = pull + links[4] * same[4] * pad_axis(centre[:, :, :, :-1], 3, 1, 0) + links[5] * same[5] * pad_axis(centre[:, :, :, 1:], 3, 0, 1)
    updated = mask * (centre - relax_weight * (diagonal * centre - pull) / diagonal)
    return updated / (lax.optimization_barrier(jnp.sum(updated, axis=0)) + outside)[None]

def apply_plain(field_ext, diagonal, links):
    centre = field_ext[1:-1]
    pull = links[0] * field_ext[:-2] + links[1] * field_ext[2:]
    pull = pull + links[2] * pad_axis(centre[:, :-1], 1, 1, 0) + links[3] * pad_axis(centre[:, 1:], 1, 0, 1)
    pull = pull + links[4] * pad_axis(centre[:, :, :-1], 2, 1, 0) + links[5] * pad_axis(centre[:, :, 1:], 2, 0, 1)
    return diagonal * centre - pull

def block_sums(field):
    length, columns, depth = field.shape
    return lax.optimization_barrier(jnp.sum(field.reshape(length // BX, BX, columns // BY, BY, depth // BZ, BZ), axis=(1, 3, 5)))

def probe_blocks(basis_ext, nodes_x, nodes_y, nodes_z, diagonal, links):
    rest_x = nodes_x % 3
    rest_y = nodes_y % 3
    rest_z = nodes_z % 3

    def one_probe(probe):
        pick = spread((rest_x == probe // 9).astype(jnp.float32), 0)
        pick = pick * spread((rest_y == probe // 3 % 3).astype(jnp.float32), 1)
        pick = pick * spread((rest_z == probe % 3).astype(jnp.float32), 2)
        field = lax.optimization_barrier(jnp.sum(basis_ext * pick, axis=0))
        return block_sums(apply_plain(field, diagonal, links))
    return lax.map(one_probe, jnp.arange(27, dtype=jnp.int32))

def coarse_matrix(probes, first_block):
    shape = probes.shape
    offsets = jnp.arange(27, dtype=jnp.int32)[:, None, None, None]
    index_x = (first_block + jnp.arange(shape[1], dtype=jnp.int32))[None, :, None, None]
    index_y = jnp.arange(shape[2], dtype=jnp.int32)[None, None, :, None]
    index_z = jnp.arange(shape[3], dtype=jnp.int32)[None, None, None, :]
    pick = (index_x + offsets // 9 - 1) % 3 * 9 + (index_y + offsets // 3 % 3 - 1) % 3 * 3 + (index_z + offsets % 3 - 1) % 3
    pick = jnp.broadcast_to(pick, shape).astype(jnp.int32)
    return jnp.take_along_axis(probes, pick, axis=0)

def coarse_apply(matrix, vector_ext):
    count_x, count_y, count_z = (matrix.shape[1], matrix.shape[2], matrix.shape[3])
    padded = pad_axis(pad_axis(vector_ext, 1, 1, 1), 2, 1, 1)
    total = jnp.zeros((count_x, count_y, count_z), jnp.float32)
    for offset in range(27):
        step_x = offset // 9
        step_y = offset // 3 % 3
        step_z = offset % 3
        total = total + matrix[offset] * padded[step_x:step_x + count_x, step_y:step_y + count_y, step_z:step_z + count_z]
    return total

def zero_rims(vector):
    return pad_axis(vector, 0, 1, 1)

def keep_pair(pair):
    return pair

def coarse_solve(matrix, rhs, extend, total_sums, count):
    weight = lax.optimization_barrier(jnp.sum(jnp.abs(matrix), axis=0))

    def apply_op(vector):
        return coarse_apply(matrix, extend(vector))
    first = apply_op(rhs) / weight
    second = apply_op(first) / weight
    sum_first, sum_second = total_sums((jnp.sum(first * first), jnp.sum(second * second)))
    spectral = jnp.sqrt(sum_second / count / (sum_first / count + tiny_eps))
    upper = upper_margin * spectral
    lower = lower_share * upper
    centre = 0.5 * (upper + lower)
    half_width = 0.5 * (upper - lower)
    ratio = centre / half_width
    damping = 1.0 / ratio
    residual = rhs
    update = residual / (weight * centre)
    solution = jnp.zeros_like(rhs)
    for sweep in range(CHEBY):
        solution = solution + update
        if sweep + 1 < CHEBY:
            residual = residual - apply_op(update)
            damping_next = 1.0 / (2.0 * ratio - damping)
            update = damping_next * damping * update + 2.0 * damping_next / half_width * residual / weight
            damping = damping_next
    return solution

def prolong(basis, solution_ext, index_x, nodes_y, nodes_z):
    padded = pad_axis(pad_axis(solution_ext, 1, 1, 1), 2, 1, 1)
    total = jnp.zeros(basis.shape[1:], jnp.float32)
    for colour in range(8):
        picked = jnp.take(padded, index_x[colour & 1], axis=0, mode='clip')
        picked = jnp.take(picked, nodes_y[colour >> 1 & 1] + 1, axis=1, mode='clip')
        picked = jnp.take(picked, nodes_z[colour >> 2 & 1] + 1, axis=2, mode='clip')
        total = total + basis[colour] * picked
    return total

def transport(pressure_ext, satur_ext, mob_ext, face_x, face_y, face_z, porosity, source):
    frac_ext = satur_ext * satur_ext / water_viscosity / mob_ext
    flow_x = face_x * (pressure_ext[:-1] - pressure_ext[1:])
    water_x = jnp.where(flow_x > 0, frac_ext[:-1], frac_ext[1:]) * flow_x
    pressure = pressure_ext[1:-1]
    fraction = frac_ext[1:-1]
    flow_y = face_y * (pressure[:, :-1] - pressure[:, 1:])
    water_y = jnp.where(flow_y > 0, fraction[:, :-1], fraction[:, 1:]) * flow_y
    flow_z = face_z * (pressure[:, :, :-1] - pressure[:, :, 1:])
    water_z = jnp.where(flow_z > 0, fraction[:, :, :-1], fraction[:, :, 1:]) * flow_z
    net_out = water_x[1:] - water_x[:-1] + pad_axis(water_y, 1, 0, 1) - pad_axis(water_y, 1, 1, 0)
    net_out = net_out + pad_axis(water_z, 2, 0, 1) - pad_axis(water_z, 2, 1, 0)
    leaving = jnp.maximum(flow_x[1:], 0.0) + jnp.maximum(-flow_x[:-1], 0.0)
    leaving = leaving + pad_axis(jnp.maximum(flow_y, 0.0), 1, 0, 1) + pad_axis(jnp.maximum(-flow_y, 0.0), 1, 1, 0)
    leaving = leaving + pad_axis(jnp.maximum(flow_z, 0.0), 2, 0, 1) + pad_axis(jnp.maximum(-flow_z, 0.0), 2, 1, 0)
    leaving = leaving + jnp.maximum(-source, 0.0)
    speed = leaving / porosity
    gain = jnp.maximum(source, 0.0) + jnp.minimum(source, 0.0) * fraction - net_out
    return (gain, speed)

def reference(log_perm, saturation, porosity, source, support_bits):
    coords_ext = jnp.arange(-1, NX + 1, dtype=jnp.int32)
    coords_y = jnp.arange(NY, dtype=jnp.int32)
    coords_z = jnp.arange(NZ, dtype=jnp.int32)
    inside_ext = ((coords_ext >= 0) & (coords_ext < NX)).astype(jnp.float32)
    face_ok = (inside_ext[:-1] * inside_ext[1:])[:, None, None]
    perm_ext = jnp.exp(pad_axis(log_perm, 0, 1, 1))
    satur_ext = pad_axis(saturation, 0, 1, 1)
    mob_ext = mobility(satur_ext)
    face_x, face_y, face_z, links, diagonal = coefficients(perm_ext, mob_ext, porosity, face_ok)
    nodes_ext = node_pair(coords_ext, BX)
    nodes_x = nodes_ext[:, 1:-1]
    nodes_y = node_pair(coords_y, BY)
    nodes_z = node_pair(coords_z, BZ)
    mask = support_mask(support_bits, valid_pair(nodes_x, NCX), valid_pair(nodes_y, NCY), valid_pair(nodes_z, NCZ), inside_ext[1:-1])
    same = same_flags(nodes_ext, nodes_y, nodes_z)
    outside = jnp.zeros((NX, 1, 1), jnp.float32)
    basis_ext = home_basis(coords_ext, coords_y, coords_z, inside_ext)
    basis = basis_ext[:, 1:-1]
    for sweep in range(JACOBI):
        basis = jacobi_sweep(basis_ext, mask, diagonal, links, same, outside)
        basis_ext = pad_axis(basis, 1, 1, 1)
    probes = probe_blocks(basis_ext, nodes_ext, nodes_y, nodes_z, diagonal, links)
    matrix = coarse_matrix(probes, 0)
    rhs = block_sums(source)
    solution = coarse_solve(matrix, rhs, zero_rims, keep_pair, NCX * NCY * NCZ)
    pressure = prolong(basis, zero_rims(solution), nodes_x + 1, nodes_y, nodes_z)
    pressure_ext = pad_axis(pressure, 0, 1, 1)
    gain, speed = transport(pressure_ext, satur_ext, mob_ext, face_x, face_y, face_z, porosity, source)
    top = jnp.max(speed)
    new_saturation = saturation + courant / top / porosity * gain
    return (pressure, new_saturation)
```

```python
import jax
import jax.numpy as jnp
from jax import lax
from jax.experimental import pallas as pl
from jax.experimental.pallas import tpu as pltpu
from jax.sharding import PartitionSpec as P

BX = 16
BY = 16
BZ = 8
CHEBY = 4
SUB = 8

oil_viscosity = 4.0
compress = 0.02
relax_weight = 2.0 / 3.0
courant = 0.5
upper_margin = 1.25
lower_share = 0.1
tiny_eps = 1e-06

HALO = 3
INNER = 2
TILE = 16

SMEM = pl.BlockSpec(memory_space=pltpu.SMEM)
VMEM = pl.BlockSpec(memory_space=pltpu.VMEM)
PARAMS = pltpu.CompilerParams(vmem_limit_bytes=24 * 2**20)


def rows_of(b):
    return slice(0, 3 * SUB) if b == 0 else slice(SUB, 4 * SUB)


def iota(shape, axis):
    return lax.broadcasted_iota(jnp.int32, shape, axis)


def mobility(satur):
    return satur * satur + (1.0 - satur) * (1.0 - satur) / oil_viscosity


def layer_ranges(width):
    blocks = width // BX
    ranges = []
    for j in range(blocks + 1):
        first = max(j * BX - 2, -1)
        last = min(j * BX + 2, width + 1)
        ranges.append((first, last, (0, 1), j, None))
        if j < blocks:
            ranges.append((j * BX + 2, j * BX + BX - 2, (j & 1,), None, j))
    return ranges


def basis_kernel(
    place, lp, sat, por, bits, src, low, high,
    basis, face_x, face_y, face_z, frac, coarse,
    inv_perm, mob, por_ext, bits_ext, share, start, acc,
):
    width, ny, nz = lp.shape
    blocks = width // BX
    first_block = place[0]
    is_first = first_block == 0
    is_last = place[1] == 1
    parity = first_block & 1

    row = iota((ny, nz), 0)
    lane = iota((ny, nz), 1)
    lane_in = lane % BZ
    z_last = lane_in == BZ - 1
    z_first = lane_in == 0
    y_last = row == BY - 1
    y_first = row == BY
    even = (lane // BZ) % 2 == 0
    zero = jnp.zeros((ny, nz), jnp.float32)

    def put(at, log_perm, satur):
        inv_perm[at] = jnp.exp(-log_perm)
        mob[at] = mobility(satur)

    for j in range(HALO):
        put(j, low[j], low[HALO + j])
        put(width + HALO + j, high[j], high[HALO + j])
    for j in range(INNER):
        por_ext[j] = low[2 * HALO + j]
        por_ext[width + INNER + j] = high[2 * HALO + j]
        bits_ext[j] = low[2 * HALO + INNER + j].astype(jnp.int32)
        bits_ext[width + INNER + j] = high[2 * HALO + INNER + j].astype(jnp.int32)

    def own_layer(x, carry):
        put(x + HALO, lp[x], sat[x])
        por_ext[x + INNER] = por[x]
        bits_ext[x + INNER] = bits[x]
        return carry

    lax.fori_loop(0, width, own_layer, 0)

    def x_face(at):
        shut = (is_first & (at < HALO)) | (is_last & (at >= width + HALO - 1))
        value = (mob[at] + mob[at + 1]) / (inv_perm[at] + inv_perm[at + 1])
        return value * jnp.where(shut, 0.0, 1.0)

    face_x[0] = x_face(0)

    def first_sweep(l, carry):
        at = l + 1
        m = mob[at]
        q = inv_perm[at]
        x_lo = face_x[at - 1]
        x_hi = x_face(at)
        face_x[at] = x_hi
        y_hi = (m + pltpu.roll(m, ny - 1, 0)) / (q + pltpu.roll(q, ny - 1, 0))
        y_hi = jnp.where(row < ny - 1, y_hi, 0.0)
        z_hi = (m + pltpu.roll(m, nz - 1, 1)) / (q + pltpu.roll(q, nz - 1, 1))
        z_hi = jnp.where(lane < nz - 1, z_hi, 0.0)
        y_lo = pltpu.roll(y_hi, 1, 0)
        z_lo = pltpu.roll(z_hi, 1, 1)
        face_y[l] = y_hi
        face_z[l] = z_hi
        x_from = at - HALO + BX
        block_first = jnp.where(x_from % BX == 0, 1.0, 0.0)
        block_last = jnp.where(x_from % BX == BX - 1, 1.0, 0.0)
        home = (x_from // BX + 1) & 1
        cross_x = x_lo * block_first + x_hi * block_last
        cross_y = jnp.where(y_last, y_hi, jnp.where(y_first, y_lo, 0.0))
        cross_z = jnp.where(z_last, z_hi, jnp.where(z_first, z_lo, 0.0))
        total = x_lo + x_hi + y_lo + y_hi + z_lo + z_hi
        inside = (
            x_lo * (1.0 - block_first)
            + x_hi * (1.0 - block_last)
            + jnp.where(y_last, 0.0, y_hi)
            + jnp.where(y_first, 0.0, y_lo)
            + jnp.where(z_last, 0.0, z_hi)
            + jnp.where(z_first, 0.0, z_lo)
        )
        scale = relax_weight / (compress * por_ext[l] + total)
        share[l] = scale
        marks = bits_ext[l]
        bit_a = jnp.where(home == parity, 1, 2)
        bit_other = 3 - bit_a
        bit_y = jnp.where(row < BY, 1, 4)
        bit_z = jnp.where(even, 1, 16)
        bit_yz = bit_y * bit_z

        def keep(value, bit):
            return jnp.where((marks & bit) != 0, value, 0.0)

        raw_h = keep(1.0 / 3.0 + scale * inside, bit_a * bit_yz)
        raw_x = keep(scale * cross_x, bit_other * bit_yz)
        raw_y = keep(scale * cross_y, bit_a * ((5 - bit_y) * bit_z))
        raw_z = keep(scale * cross_z, bit_a * (bit_y * (17 - bit_z)))
        outside = (is_first & (l < INNER)) | (is_last & (l >= width + INNER))
        norm = 1.0 / (raw_h + raw_x + raw_y + raw_z + jnp.where(outside, 1.0, 0.0))
        at_h = raw_h * norm
        at_x = raw_x * norm
        at_y = raw_y * norm
        at_z = raw_z * norm
        away = 1 - home
        rim = zero[:SUB]
        for c in range(2):
            here = even if c == 0 else ~even
            part_z = jnp.where(here, at_h, at_z)
            part_y = jnp.where(here, at_y, 0.0)
            part_x = jnp.where(here, at_x, 0.0)
            for a, main, side in ((home, part_z, part_y), (away, part_x, zero)):
                start[a, 0, c, l, 0:8] = rim
                start[a, 0, c, l, 8:24] = main[0:16]
                start[a, 0, c, l, 24:32] = side[16:24]
                start[a, 0, c, l, 32:40] = rim
                start[a, 1, c, l, 0:8] = rim
                start[a, 1, c, l, 8:16] = side[8:16]
                start[a, 1, c, l, 16:32] = main[16:32]
                start[a, 1, c, l, 32:40] = rim
        return carry

    lax.fori_loop(0, width + 2 * INNER, first_sweep, 0)

    def second_sweep(parities):
        def body(n, carry):
            l = n + INNER - 1
            x_lo = face_x[n + HALO - 2]
            x_hi = face_x[n + HALO - 1]
            y_hi = face_y[l]
            z_hi = face_z[l]
            y_lo = pltpu.roll(y_hi, 1, 0)
            z_lo = pltpu.roll(z_hi, 1, 1)
            scale = share[l]
            marks = bits_ext[l]
            raws = {}
            for a in parities:
                for b in range(2):
                    r = rows_of(b)
                    for c in range(2):
                        mid = start[a, b, c, l, 8:32]
                        pull = x_lo[r] * start[a, b, c, l - 1, 8:32]
                        pull = pull + x_hi[r] * start[a, b, c, l + 1, 8:32]
                        pull = pull + y_lo[r] * start[a, b, c, l, 7:31]
                        pull = pull + y_hi[r] * start[a, b, c, l, 9:33]
                        pull = pull + z_lo[r] * pltpu.roll(mid, 1, 1)
                        pull = pull + z_hi[r] * pltpu.roll(mid, nz - 1, 1)
                        bit = jnp.where(parity == a, 1 << (2 * b + 4 * c), 2 << (2 * b + 4 * c))
                        raws[a, b, c] = jnp.where(
                            (marks[r] & bit) != 0, mid * (1.0 / 3.0) + scale[r] * pull, 0.0
                        )
            outside = (is_first & (n < 1)) | (is_last & (n > width))
            rest = jnp.where(outside, 1.0, 0.0)
            norms = []
            for t in range(4):
                total = rest
                for (a, b, c), raw in raws.items():
                    at = t - b
                    if 0 <= at < 3:
                        total = total + raw[at * SUB : (at + 1) * SUB]
                norms.append(1.0 / total)
            for (a, b, c), raw in raws.items():
                for at in range(3):
                    cut = slice(at * SUB, (at + 1) * SUB)
                    basis[a, b, c, n, cut] = raw[cut] * norms[at + b]
            return carry

        return body

    for first, last, parities, _, _ in layer_ranges(width):
        lax.fori_loop(first + 1, last + 1, second_sweep(parities), 0)

    def add_layer(sums, x, a):
        l = x + INNER
        y_hi = face_y[l]
        z_hi = face_z[l]
        y_lo = pltpu.roll(y_hi, 1, 0)
        z_lo = pltpu.roll(z_hi, 1, 1)
        cross_y = jnp.where(y_last, y_hi, jnp.where(y_first, y_lo, 0.0))
        cross_z = jnp.where(z_last, z_hi, jnp.where(z_first, z_lo, 0.0))
        whole = compress * por_ext[l] + cross_y + cross_z
        out = []
        for n, (b, c) in enumerate(((0, 0), (0, 1), (1, 0), (1, 1))):
            r = rows_of(b)
            value = basis[a, b, c, x + 1]
            main, side_z, side_y = sums[3 * n : 3 * n + 3]
            middle = value[8:24] if b == 0 else value[0:16]
            out.append(main + whole[r] * value)
            out.append(side_z + cross_z[r] * value)
            out.append(side_y + cross_y[8:24] * middle)
        return tuple(out)

    def no_sums():
        one = (jnp.zeros((24, nz), jnp.float32),) * 2 + (jnp.zeros((16, nz), jnp.float32),)
        return one * 4

    def cross_x_layer(sums, a, x, other, at):
        out = list(sums)
        for n, (b, c) in enumerate(((0, 0), (0, 1), (1, 0), (1, 1))):
            gap = basis[a, b, c, x + 1] - basis[a, b, c, other + 1]
            out[3 * n] = out[3 * n] + face_x[at][rows_of(b)] * gap
        return tuple(out)

    acc[...] = jnp.zeros_like(acc)
    for j in range(blocks):
        own = j & 1
        base = j * BX
        end = base + BX - 1
        half = BX // 2
        halves = []
        for lower in (base, base + half):
            halves.append(
                lax.fori_loop(
                    lower, lower + half, lambda x, sums: add_layer(sums, x, own), no_sums()
                )
            )
        halves[0] = cross_x_layer(halves[0], own, base, base - 1, base + HALO - 1)
        halves[1] = cross_x_layer(halves[1], own, end, end + 1, end + HALO)
        below = add_layer(add_layer(no_sums(), base, 1 - own), base + 1, 1 - own)
        below = cross_x_layer(below, 1 - own, base, base - 1, base + HALO - 1)
        above = add_layer(add_layer(no_sums(), end, 1 - own), end - 1, 1 - own)
        above = cross_x_layer(above, 1 - own, end, end + 1, end + HALO)
        middle = tuple(p + q for p, q in zip(halves[0], halves[1]))

        def rhs_layer(x, sums):
            value = src[x]
            return (sums[0] + value[0:8] + value[8:16], sums[1] + value[16:24] + value[24:32])

        blank = jnp.zeros((SUB, nz), jnp.float32)
        rhs = lax.fori_loop(base, base + BX, rhs_layer, (blank, blank))
        for o, sums in enumerate((below, middle, above)):
            for c in range(2):
                p0, u0, v0 = sums[3 * c : 3 * c + 3]
                p1, u1, v1 = sums[6 + 3 * c : 9 + 3 * c]
                mains = (
                    p0[0:8] + p0[8:16] - v0[8:16],
                    p1[0:8] - v1[8:16],
                    p0[16:24] - v0[0:8],
                    p1[8:16] + p1[16:24] - v1[0:8],
                )
                sides = (u0[0:8] + u0[8:16], u1[0:8], u0[16:24], u1[8:16] + u1[16:24])
                for k in range(4):
                    n = 4 * o + k
                    acc[(c * TILE + n) * SUB : (c * TILE + n + 1) * SUB] = mains[k]
                    acc[((2 + c) * TILE + n) * SUB : ((2 + c) * TILE + n + 1) * SUB] = sides[k]
        for c in range(2):
            for k in range(2):
                n = c * TILE + 12 + k
                acc[n * SUB : (n + 1) * SUB] = rhs[k]

        def gather(group):
            total = acc[pl.ds(group * TILE * SUB, TILE, stride=SUB), :]
            for s in range(1, SUB):
                total = total + acc[pl.ds(group * TILE * SUB + s, TILE, stride=SUB), :]
            return total

        lane_t = iota((TILE, nz), 1)
        in_t = lane_t % BZ
        even_t = (lane_t // BZ) % 2 == 0
        parts = []
        for c in range(2):
            side = gather(2 + c)
            part = gather(c)
            part = part - jnp.where(in_t == BZ - 1, pltpu.roll(side, nz - 1, 1), 0.0)
            part = part - jnp.where(in_t == 0, pltpu.roll(side, 1, 1), 0.0)
            parts.append(part)

        def fours(value):
            value = value + pltpu.roll(value, nz - 1, 1)
            return value + pltpu.roll(value, nz - 2, 1)

        same = fours(jnp.where(even_t, parts[0], parts[1]))
        same = same + pltpu.roll(same, nz - BZ // 2, 1)
        beside = fours(jnp.where(even_t, parts[1], parts[0]))
        packed = jnp.where(in_t % (BZ // 2) == 0, beside, 0.0)
        coarse[j * TILE : (j + 1) * TILE] = jnp.where(in_t == 1, pltpu.roll(same, 1, 1), packed)

    def fraction(x, carry):
        at = x + HALO
        frac[x + 1] = carry_sat(x) / mob[at]
        return carry

    def carry_sat(x):
        value = sat[x]
        return value * value

    frac[0] = low[2 * HALO - 1] * low[2 * HALO - 1] / mob[HALO - 1]
    frac[width + 1] = high[HALO] * high[HALO] / mob[width + HALO]
    lax.fori_loop(0, width, fraction, 0)


def flow_kernel(
    place, gathered, basis, face_x, face_y, face_z, frac, por, src, pressure, gain, top, sol, press
):
    width, ny, nz = por.shape
    blocks = width // BX
    count_x = gathered.shape[0] // TILE
    count = count_x * (ny // BY) * (nz // BZ)
    first_block = place[0]
    lane_c = iota((count_x, nz), 1)
    at_node = lane_c % BZ == 0

    matrix = {}
    for o in range(3):
        for k in range(4):
            line = gathered[pl.ds(4 * o + k, count_x, stride=TILE), :]
            for z, shift in ((0, 0), (1, 1), (2, BZ // 2)):
                value = pltpu.roll(line, nz - shift, 1) if shift else line
                matrix[k, o, z] = jnp.where(at_node, value, 0.0)
    rhs = tuple(
        jnp.where(at_node, pltpu.roll(gathered[pl.ds(12 + k, count_x, stride=TILE), :], nz - 1, 1), 0.0)
        for k in range(2)
    )
    rows = ((0, 1), (3, 2))

    def weight_of(iy):
        total = jnp.where(at_node, 0.0, 1.0)
        for k in rows[iy]:
            for o in range(3):
                for z in range(3):
                    total = total + jnp.abs(matrix[k, o, z])
        return total

    weight = (weight_of(0), weight_of(1))
    inverse = (1.0 / weight[0], 1.0 / weight[1])

    def apply_op(vector):
        moved = []
        for iy in range(2):
            shifts = {}
            for o in range(3):
                v = vector[iy] if o == 1 else pltpu.roll(vector[iy], (1 - o) % count_x, 0)
                for z in range(3):
                    shifts[o, z] = v if z == 1 else pltpu.roll(v, (1 - z) * BZ % nz, 1)
            moved.append(shifts)
        out = []
        for iy in range(2):
            total = None
            for k, shifts in zip(rows[iy], (moved[iy], moved[1 - iy])):
                for o in range(3):
                    for z in range(3):
                        term = matrix[k, o, z] * shifts[o, z]
                        total = term if total is None else total + term
            out.append(total)
        return tuple(out)

    def mean_square(vector):
        both = vector[0] * vector[0] + vector[1] * vector[1]
        return jnp.sum(jnp.sum(both, axis=0, keepdims=True), axis=1, keepdims=True) / count

    first = tuple(v * w for v, w in zip(apply_op(rhs), inverse))
    second = tuple(v * w for v, w in zip(apply_op(first), inverse))
    spectral = jnp.sqrt(mean_square(second) / (mean_square(first) + tiny_eps))
    upper = upper_margin * spectral
    lower = lower_share * upper
    centre = 0.5 * (upper + lower)
    half_width = 0.5 * (upper - lower)
    ratio = centre / half_width
    damping = 1.0 / ratio
    residual = rhs
    by_centre = 1.0 / centre
    update = tuple(r * w * by_centre for r, w in zip(residual, inverse))
    total = (jnp.zeros_like(rhs[0]),) * 2
    for sweep in range(CHEBY):
        total = tuple(t + u for t, u in zip(total, update))
        if sweep + 1 < CHEBY:
            applied = apply_op(update)
            residual = tuple(r - a for r, a in zip(residual, applied))
            following = 1.0 / (2.0 * ratio - damping)
            old = following * damping
            new = 2.0 * following / half_width
            update = tuple(
                old * u + new * (r * w) for u, r, w in zip(update, residual, inverse)
            )
            damping = following

    in_c = lane_c % BZ
    even_c = (lane_c // BZ) % 2 == 0
    rim = jnp.zeros((SUB, nz), jnp.float32)
    for b in range(2):
        own = total[b]
        for step in (1, 2, 4):
            own = own + pltpu.roll(own, step, 1)
        beside = jnp.where(in_c < BZ // 2, pltpu.roll(own, BZ, 1), pltpu.roll(own, nz - BZ, 1))
        for c, value in enumerate((jnp.where(even_c, own, beside), jnp.where(even_c, beside, own))):
            sol[b, c, 0:SUB] = rim
            sol[b, c, SUB : SUB + count_x] = value
            sol[b, c, SUB + count_x : 2 * SUB + count_x] = rim

    def prolong(parities, block_of):
        nodes = {}
        for a in parities:
            for b in range(2):
                for c in range(2):
                    nodes[a, b, c] = jnp.broadcast_to(
                        sol[b, c, pl.ds(SUB + first_block + block_of(a), 1), :], (SUB, nz)
                    )

        def body(n, carry):
            parts = [None] * 4
            for (a, b, c), node in nodes.items():
                value = basis[a, b, c, n]
                for at in range(3):
                    term = value[at * SUB : (at + 1) * SUB] * node
                    t = at + b
                    parts[t] = term if parts[t] is None else parts[t] + term
            for t in range(4):
                press[n, (t + 1) * SUB : (t + 2) * SUB] = parts[t]
            press[n, 5 * SUB : 6 * SUB] = rim
            return carry

        return body

    for start, stop, parities, interface, block in layer_ranges(width):
        if interface is None:
            block_of = lambda a, block=block: block
        else:
            block_of = lambda a, j=interface: j if a == (j & 1) else j - 1
        lax.fori_loop(start + 1, stop + 1, prolong(parities, block_of), 0)

    cells = slice(SUB, SUB + ny)

    def across_x(x):
        flow = face_x[x + HALO] * (press[x + 1, cells] - press[x + 2, cells])
        return flow, jnp.where(flow > 0, frac[x + 1], frac[x + 2]) * flow

    def transport(x, carry):
        flow_lo, water_lo, largest = carry
        flow_hi, water_hi = across_x(x)
        p = press[x + 1, cells]
        f = frac[x + 1]
        flow_y = face_y[x + INNER] * (p - press[x + 1, SUB + 1 : SUB + 1 + ny])
        water_y = jnp.where(flow_y > 0, f, pltpu.roll(f, ny - 1, 0)) * flow_y
        flow_z = face_z[x + INNER] * (p - pltpu.roll(p, nz - 1, 1))
        water_z = jnp.where(flow_z > 0, f, pltpu.roll(f, nz - 1, 1)) * flow_z
        net_out = water_hi - water_lo + water_y - pltpu.roll(water_y, 1, 0)
        net_out = net_out + water_z - pltpu.roll(water_z, 1, 1)
        s = src[x]
        leaving = jnp.maximum(flow_hi, 0.0) + jnp.maximum(-flow_lo, 0.0)
        leaving = leaving + jnp.maximum(flow_y, 0.0) + pltpu.roll(jnp.maximum(-flow_y, 0.0), 1, 0)
        leaving = leaving + jnp.maximum(flow_z, 0.0) + pltpu.roll(jnp.maximum(-flow_z, 0.0), 1, 1)
        leaving = leaving + jnp.maximum(-s, 0.0)
        by_pore = 1.0 / por[x]
        pressure[x] = p
        gain[x] = (jnp.maximum(s, 0.0) + jnp.minimum(s, 0.0) * f - net_out) * by_pore
        return flow_hi, water_hi, jnp.maximum(largest, leaving * by_pore)

    flow, water = across_x(-1)
    _, _, largest = lax.fori_loop(
        0, width, transport, (flow, water, jnp.zeros((ny, nz), jnp.float32))
    )
    top[...] = jnp.maximum(
        jnp.maximum(largest[0:8], largest[8:16]), jnp.maximum(largest[16:24], largest[24:32])
    )


def step_kernel(*refs):
    tops, (sat, gain, out) = refs[:-3], refs[-3:]
    top = tops[0][...]
    for other in tops[1:]:
        top = jnp.maximum(top, other[...])
    top = jnp.max(jnp.max(top, axis=0, keepdims=True), axis=1, keepdims=True)
    step = courant / top
    out[...] = sat[...] + step[None] * gain[...]


def radices(count):
    out = []
    while count > 1:
        radix = next(r for r in (4, 3, 2, count) if count % r == 0)
        out.append(radix)
        count //= radix
    return out


def digit_pairs(count, stride, radix, step):
    pairs = []
    for i in range(count):
        digit = i // stride % radix
        pairs.append((i, i + ((digit + step) % radix - digit) * stride))
    return pairs


def gather_all(block, axis):
    count = lax.axis_size(axis)
    index = lax.axis_index(axis)
    stride = 1
    whole = block[None]
    for radix in radices(count):
        parts = [whole] + [
            lax.ppermute(whole, axis, digit_pairs(count, stride, radix, step))
            for step in range(1, radix)
        ]
        digit = index // stride % radix
        order = (digit - jnp.arange(radix, dtype=jnp.int32)) % radix
        joined = jnp.stack(parts)
        joined = jnp.take(joined, order, axis=0)
        whole = joined.reshape((-1,) + block.shape)
        stride *= radix
    return whole.reshape((-1,) + block.shape[1:])


def largest_all(tile, axis):
    count = lax.axis_size(axis)
    stride = 1
    parts = [tile]
    for radix in radices(count):
        tile = parts[0]
        for other in parts[1:]:
            tile = jnp.maximum(tile, other)
        parts = [tile] + [
            lax.ppermute(tile, axis, digit_pairs(count, stride, radix, step))
            for step in range(1, radix)
        ]
        stride *= radix
    return parts


def on_device(log_perm, saturation, porosity, source, support_bits):
    width, ny, nz = log_perm.shape
    devices = lax.axis_size("gx")
    f32 = jnp.float32

    def rim(cut):
        marks = support_bits[cut(INNER)].astype(f32)
        return jnp.concatenate(
            [log_perm[cut(HALO)], saturation[cut(HALO)], porosity[cut(INNER)], marks]
        )

    forward = [(i, i + 1) for i in range(devices - 1)]
    backward = [(i + 1, i) for i in range(devices - 1)]
    low = lax.ppermute(rim(lambda n: slice(width - n, width)), "gx", forward)
    high = lax.ppermute(rim(lambda n: slice(0, n)), "gx", backward)

    blocks = width // BX
    position = lax.axis_index("gx")
    place = jnp.stack([position * blocks, (position == devices - 1).astype(jnp.int32)])
    ext = width + 2 * HALO
    mid = width + 2 * INNER
    basis, face_x, face_y, face_z, frac, coarse = pl.pallas_call(
        basis_kernel,
        out_shape=(
            jax.ShapeDtypeStruct((2, 2, 2, width + 2, 24, nz), f32),
            jax.ShapeDtypeStruct((ext - 1, ny, nz), f32),
            jax.ShapeDtypeStruct((mid, ny, nz), f32),
            jax.ShapeDtypeStruct((mid, ny, nz), f32),
            jax.ShapeDtypeStruct((width + 2, ny, nz), f32),
            jax.ShapeDtypeStruct((blocks * TILE, nz), f32),
        ),
        in_specs=[SMEM] + [VMEM] * 7,
        out_specs=(VMEM,) * 6,
        scratch_shapes=[
            pltpu.VMEM((ext, ny, nz), f32),
            pltpu.VMEM((ext, ny, nz), f32),
            pltpu.VMEM((mid, ny, nz), f32),
            pltpu.VMEM((mid, ny, nz), jnp.int32),
            pltpu.VMEM((mid, ny, nz), f32),
            pltpu.VMEM((2, 2, 2, mid, 40, nz), f32),
            pltpu.VMEM((4 * TILE * SUB, nz), f32),
        ],
        compiler_params=PARAMS,
        name="basis",
    )(place, log_perm, saturation, porosity, support_bits, source, low, high)
    gathered = gather_all(coarse, "gx")
    pressure, gain, top = pl.pallas_call(
        flow_kernel,
        out_shape=(
            jax.ShapeDtypeStruct((width, ny, nz), f32),
            jax.ShapeDtypeStruct((width, ny, nz), f32),
            jax.ShapeDtypeStruct((SUB, nz), f32),
        ),
        in_specs=[SMEM] + [VMEM] * 8,
        out_specs=(VMEM,) * 3,
        scratch_shapes=[
            pltpu.VMEM((2, 2, devices * blocks + 2 * SUB, nz), f32),
            pltpu.VMEM((width + 2, ny + 2 * SUB, nz), f32),
        ],
        compiler_params=PARAMS,
        name="flow",
    )(place, gathered, basis, face_x, face_y, face_z, frac, porosity, source)
    tops = largest_all(top, "gx")
    new_saturation = pl.pallas_call(
        step_kernel,
        out_shape=jax.ShapeDtypeStruct((width, ny, nz), f32),
        in_specs=[VMEM] * (len(tops) + 2),
        out_specs=VMEM,
        compiler_params=PARAMS,
        name="step",
    )(*tops, saturation, gain)
    return (pressure, new_saturation)


def solution(mesh):
    placed = P(("groups", "gx"), None, None)
    return jax.shard_map(
        on_device,
        mesh=mesh,
        in_specs=(placed,) * 5,
        out_specs=(placed, placed),
        check_vma=False,
    )
```
